512 devices in a mesh: lon: 64 (over y, z_hi, x, core), tm: 8 (over z_lo).
Axes of the slice: x: 4, y: 4, z: 16 (z_hi: 2, z_lo: 8; z = z_hi * 8 + z_lo), core: 2. Of those that a mesh axis runs over, the one named last changes fastest.
Arguments:
- queries: bfloat16 [8, 256, 32, 1024], P('tm', 'lon'), may hold values from -8 to 8
- token_keys: bfloat16 [8, 256, 32, 1024], P('tm', 'lon'), may hold values from -8 to 8
- values: bfloat16 [8, 256, 32, 1024], P('tm', 'lon'), may hold values from -6 to 6
- grad_out: bfloat16 [8, 256, 32, 1024], P('tm', 'lon'), may hold values from -6 to 6
- window_shifts: int32 [8, 2], replicated, may hold values from 0 to 7
- noise_steps: int32 [8], replicated, may hold values from 0 to 63
- gate_table: float32 [64, 1024], replicated, may hold values from -4 to 4
Outputs:
- d_queries: bfloat16 [8, 256, 32, 1024], P('tm', 'lon')
- d_keys: bfloat16 [8, 256, 32, 1024], P('tm', 'lon')
- d_values: bfloat16 [8, 256, 32, 1024], P('tm', 'lon')
The draws below stay inside these ranges and needn't reach their ends.
All inputs are finite; a program needn't handle non-finite values.
Results may differ from the reference program's by a relative error of at most 0.0073.
Values may be sent and summed in bfloat16 or wider, within the bound.
No kernel may reach another device: no remote copies, remote signals or barrier semaphores. Data moves between devices by JAX's collectives and lax.ppermute only.
A program may use at most 64 MiB of HBM per device.

```python
import jax
import jax.numpy as jnp
from jax import lax

HEADS = 16
HEAD_DIM = 64
D = 1024
WIN = 8
LAT = 32
LEVELS = 64
FRAMES = 8
LON = 256


def draw_queries(key, part):
    key = jax.random.fold_in(key, 101)
    drawn = jnp.clip(jax.random.normal(key, (FRAMES, LON, LAT, D), jnp.float32), -6.0, 6.0)
    return drawn.astype(jnp.bfloat16)


def draw_token_keys(key, part):
    key = jax.random.fold_in(key, 202)
    drawn_key = jax.random.fold_in(key, 0)
    drawn = jnp.clip(jax.random.normal(drawn_key, (FRAMES, LON, LAT, D), jnp.float32), -6.0, 6.0)
    return drawn.astype(jnp.bfloat16)


def set_ends(values, rng, least, top_value):
    shape = values.shape
    spot = [jax.random.randint(jax.random.fold_in(rng, axis), (), 0, shape[axis]) for axis in range(len(shape))]
    values = values.at[tuple(spot)].set(least)
    longest = shape.index(max(shape))
    spot[longest] = (spot[longest] + 1) % shape[longest]
    return values.at[tuple(spot)].set(top_value)


def block_scale(rng, dims, cuts, least, high):
    gain, own = 1.0, jax.random.fold_in(rng, 6)
    for axis_at, parts in cuts:
        steps = jnp.exp(jax.random.uniform(jax.random.fold_in(own, axis_at), (parts,), jnp.float32, least / len(cuts), high / len(cuts)))
        gain = gain * jnp.repeat(steps, dims[axis_at] // parts).reshape([-1 if axis == axis_at else 1 for axis in range(len(dims))])
    return gain


def normal_values(key, extent, spread, reach, cuts=(), kind=jnp.bfloat16):
    level = block_scale(key, extent, cuts, -0.22, 0.18) if cuts else 1.0
    result = jax.random.normal(key, extent, jnp.float32) * spread * level
    return jnp.minimum(jnp.maximum(result, -reach), reach).astype(kind)


def setup_inputs(seed: int = 0) -> dict:
    streams_of = jax.random.split(jax.random.key(seed), 8)
    queries = draw_queries(jax.random.fold_in(streams_of[7], 71), 0)
    token_keys = draw_token_keys(jax.random.fold_in(streams_of[7], 71), 0)
    values = normal_values(streams_of[2], (FRAMES, LON, LAT, D), 1.0, 6.0, ((0, 8), (1, 64)))
    grad_out = normal_values(streams_of[3], (FRAMES, LON, LAT, D), 1.0, 6.0, ((0, 8), (1, 64)))
    window_shifts = set_ends(jax.random.randint(streams_of[4], (FRAMES, 2), 0, WIN), jax.random.fold_in(streams_of[4], 1), 0, WIN - 1).astype(jnp.int32)
    noise_steps = set_ends(jax.random.randint(streams_of[5], (FRAMES,), 0, LEVELS), jax.random.fold_in(streams_of[5], 1), 0, LEVELS - 1).astype(jnp.int32)
    gate_table = normal_values(streams_of[6], (LEVELS, D), 1.0, 4.0, (), jnp.float32)
    return dict(queries=queries, token_keys=token_keys, values=values, grad_out=grad_out, window_shifts=window_shifts, noise_steps=noise_steps, gate_table=gate_table)


neg_large = -1e30


def to_windows(field, lat_shift):
    columns = field.shape[0]
    blocks = LAT // WIN + 1
    padded = jnp.pad(field, ((0, 0), (WIN, WIN), (0, 0)))
    picked = lax.dynamic_slice_in_dim(padded, lat_shift, blocks * WIN, 1)
    picked = picked.reshape(columns, blocks, WIN, field.shape[2]).transpose(1, 0, 2, 3)
    return picked.reshape(blocks, columns * WIN, field.shape[2])


def from_windows(tiles, lat_shift, columns):
    blocks = LAT // WIN + 1
    whole = tiles.reshape(blocks, columns, WIN, tiles.shape[2]).transpose(1, 0, 2, 3)
    whole = whole.reshape(columns, blocks * WIN, tiles.shape[2])
    return lax.dynamic_slice_in_dim(whole, WIN - lat_shift, LAT, 1)


def row_valid(lat_shift, columns):
    blocks = LAT // WIN + 1
    latitude = jnp.arange(blocks * WIN, dtype=jnp.int32) - WIN + lat_shift
    inside = ((latitude >= 0) & (latitude < LAT)).reshape(blocks, 1, WIN)
    return jnp.broadcast_to(inside, (blocks, columns, WIN)).reshape(blocks, columns * WIN)


def narrowed(field):
    return lax.optimization_barrier(field.astype(jnp.bfloat16)).astype(jnp.float32)


def attend_grads(query_heads, key_heads, value_heads, grad_heads, allowed):
    scaling = HEAD_DIM ** -0.5
    scores = jnp.einsum('...qnd,...knd->...nqk', query_heads, key_heads) * scaling
    row_max = jnp.max(jnp.where(allowed, scores, neg_large), axis=-1, keepdims=True)
    row_sum = jnp.sum(jnp.where(allowed, jnp.exp(scores - row_max), 0.0), axis=-1, keepdims=True)
    log_total = row_max + jnp.log(jnp.maximum(row_sum, 1.0))
    weights = jnp.where(allowed, jnp.exp(scores - log_total), 0.0)
    dweights = jnp.einsum('...qnd,...knd->...nqk', grad_heads, value_heads)
    row_delta = jnp.sum(weights * dweights, axis=-1, keepdims=True)
    dscores = narrowed(weights * (dweights - row_delta))
    low_weights = narrowed(weights)
    grad_query = jnp.einsum('...nqk,...knd->...qnd', dscores, key_heads) * scaling
    grad_key = jnp.einsum('...nqk,...qnd->...knd', dscores, query_heads) * scaling
    grad_value = jnp.einsum('...nqk,...qnd->...knd', low_weights, grad_heads)
    return grad_query, grad_key, grad_value


def spatial_frame(inputs):
    query_frame, key_frame, value_frame, grad_frame, shift_pair = inputs
    lat_shift = shift_pair[0]
    lon_shift = shift_pair[1]
    groups = LON // WIN
    blocks = LAT // WIN + 1

    def prepare(field):
        rolled = jnp.roll(field, -lon_shift, axis=0).reshape(groups, WIN, LAT, D)
        tiles = jax.vmap(lambda strip: to_windows(strip, lat_shift))(rolled)
        return tiles.reshape(groups, blocks, WIN * WIN, HEADS, HEAD_DIM)

    allowed = row_valid(lat_shift, WIN)[:, None, None, :]
    grads = attend_grads(prepare(query_frame), prepare(key_frame), prepare(value_frame), prepare(grad_frame), allowed)

    def restore(tiles):
        tiles = tiles.reshape(groups, blocks, WIN * WIN, D)
        strips = jax.vmap(lambda strip: from_windows(strip, lat_shift, WIN))(tiles)
        return jnp.roll(strips.reshape(LON, LAT, D), lon_shift, axis=0)

    return (restore(grads[0]), restore(grads[1]), restore(grads[2]))


def temporal_grads(query_wide, key_wide, value_wide, grad_t):
    positions = LON * LAT

    def heads_of(field):
        return field.reshape(FRAMES, positions, HEADS, HEAD_DIM).transpose(1, 0, 2, 3)

    def restore(field):
        return narrowed(field.transpose(1, 0, 2, 3).reshape(FRAMES, LON, LAT, D))

    allowed = jnp.ones((1, 1, 1), dtype=bool)
    grads = attend_grads(heads_of(query_wide), heads_of(key_wide), heads_of(value_wide), heads_of(grad_t), allowed)
    return (restore(grads[0]), restore(grads[1]), restore(grads[2]))


def reference(queries, token_keys, values, grad_out, window_shifts, noise_steps, gate_table):
    query_wide = queries.astype(jnp.float32)
    key_wide = token_keys.astype(jnp.float32)
    value_wide = values.astype(jnp.float32)
    grad_wide = grad_out.astype(jnp.float32)
    spatial = lax.map(spatial_frame, (query_wide, key_wide, value_wide, grad_wide, window_shifts))
    gating = gate_table[noise_steps]
    grad_t = narrowed(grad_wide * gating[:, None, None, :])
    temporal = temporal_grads(query_wide, key_wide, value_wide, grad_t)
    return ((spatial[0] + temporal[0]).astype(jnp.bfloat16),
            (spatial[1] + temporal[1]).astype(jnp.bfloat16),
            (spatial[2] + temporal[2]).astype(jnp.bfloat16))
```

```python
import jax
import jax.numpy as jnp
from jax import lax
from jax.experimental import pallas as pl
from jax.experimental.pallas import tpu as pltpu
from jax.sharding import PartitionSpec as P

HEAD_DIM = 64
WIN = 8
LANES = 128
PAIRS = 4
SLOTS = 9
HALF = 5
ROW = 4
SCALE = HEAD_DIM**-0.5
NEG = -1e30
VMEM = pl.BlockSpec(memory_space=pltpu.VMEM)
SMEM = pl.BlockSpec(memory_space=pltpu.SMEM)
ANY = pl.BlockSpec(memory_space=pl.ANY)
SPATIAL_FLOPS = 480 << 26
TEMPORAL_FLOPS = 1 << 20
GATHER_FLOPS = 84 << 28
BF16 = jnp.bfloat16
F32 = jnp.float32


def low_pairs(b):
    one = jnp.int32(1)
    zero = jnp.int32(0)
    return sum(jnp.where(b < top, one, zero) for top in (2, 4, 5, 7))


def call(body, outs, in_specs, flops, nbytes, scratch=(), mib=48):
    return pl.pallas_call(
        body,
        out_shape=[jax.ShapeDtypeStruct(s, BF16) for s in outs],
        in_specs=in_specs,
        out_specs=[VMEM] * len(outs),
        scratch_shapes=list(scratch),
        compiler_params=pltpu.CompilerParams(vmem_limit_bytes=mib << 20),
        cost_estimate=pl.CostEstimate(flops=flops, bytes_accessed=nbytes, transcendentals=0),
    )


def split_body(scal, q, k, v, g, stacked, own, other, held, sems):
    core = scal[2]
    copies = [pltpu.make_async_copy(ref, held.at[r], sems.at[r]) for r, ref in enumerate((q, k, v, g))]
    for copy in copies:
        copy.start()
    for r, copy in enumerate(copies):
        copy.wait()
        for i in range(8):
            stacked[i, 16 * r : 16 * r + 16, :] = held[r, 16 * i : 16 * i + 16, :]
        for half in range(2):

            @pl.when(core == half)
            def _(r=r, half=half):
                for p in range(PAIRS):
                    lo = half * PAIRS * LANES + p * LANES
                    hi = (1 - half) * PAIRS * LANES + p * LANES
                    own[r, p] = held[r, :, lo : lo + LANES].reshape(4, 32, LANES)
                    other[r, p] = held[r, :, hi : hi + LANES].reshape(4, 32, LANES)


def row_end(scal):
    return scal[3] == 0, scal[3] == 3


def store_block(slot, count, block, side, cross_a, cross_b, crosses):
    for r in range(count):
        side[r, slot] = block(r)

    @pl.when(jnp.logical_and(crosses, slot < HALF))
    def _():
        for r in range(count):
            cross_a[r, slot] = block(r)

    @pl.when(jnp.logical_and(crosses, slot >= HALF))
    def _():
        for r in range(count):
            cross_b[r, slot - HALF] = block(r)


def load_block(slot, count, put, side, cross_a, cross_b, crosses):
    @pl.when(jnp.logical_not(crosses))
    def _():
        for r in range(count):
            put(r, side[r, slot])

    @pl.when(jnp.logical_and(crosses, slot < HALF))
    def _():
        for r in range(count):
            put(r, cross_a[r, slot])

    @pl.when(jnp.logical_and(crosses, slot >= HALF))
    def _():
        for r in range(count):
            put(r, cross_b[r, slot - HALF])


def halo_body(scal, own, got, whole, to_left, to_right, cross_a, cross_b):
    b = scal[1]
    core = scal[2]
    first, last = row_end(scal)
    n_low = low_pairs(b)
    for r in range(4):
        for p in range(PAIRS):
            whole[r, p, pl.ds(core * 4, 4)] = own[r, p]
            whole[r, p, pl.ds((1 - core) * 4, 4)] = got[r, p]
    for p in range(PAIRS):

        @pl.when(p < n_low)
        def _(p=p):
            def put(col, carry):
                block = lambda r: whole[r, p, col]
                store_block(p * b + col, 4, block, to_left, cross_a, cross_b, first)
                return carry

            lax.fori_loop(0, b, put, 0)

        @pl.when(p >= n_low)
        def _(p=p):
            def put(col, carry):
                block = lambda r: whole[r, p, col]
                slot = (p - n_low) * (8 - b) + col - b
                store_block(slot, 4, block, to_right, cross_a, cross_b, last)
                return carry

            lax.fori_loop(b, 8, put, 0)


def attend(q, k, v, g, mask):
    tokens = q.shape[0]
    lane = lax.broadcasted_iota(jnp.int32, (1, LANES), 1)
    first = jnp.where(lane < HEAD_DIM, 1.0, 0.0).astype(BF16)
    second = jnp.where(lane < HEAD_DIM, 0.0, 1.0).astype(BF16)
    q = q * jnp.asarray(SCALE, BF16)
    q2 = jnp.concatenate([q * first, q * second], axis=0)
    g2 = jnp.concatenate([g * first, g * second], axis=0)
    over_last = (((1,), (1,)), ((), ()))
    over_first = (((0,), (0,)), ((), ()))
    s = lax.dot_general(q2, k, over_last, preferred_element_type=F32)
    dp = lax.dot_general(g2, v, over_last, preferred_element_type=F32)
    s = jnp.where(mask, s, NEG)
    e = jnp.exp(s - jnp.max(s, axis=1, keepdims=True))
    p = e * (1.0 / jnp.sum(e, axis=1, keepdims=True))
    delta = jnp.sum(p * dp, axis=1, keepdims=True)
    ds = (p * (dp - delta)).astype(BF16)
    p = p.astype(BF16)
    dv = lax.dot_general(p, g2, over_first, preferred_element_type=F32)
    dk = lax.dot_general(ds, q2, over_first, preferred_element_type=F32)
    dq = jnp.dot(ds[:tokens], k * first, preferred_element_type=F32)
    dq = dq + jnp.dot(ds[tokens:], k * second, preferred_element_type=F32)
    return (dq * SCALE, dk, dv)


def spatial_body(
    scal, whole, from_left, from_right, in_a, in_b,
    local, back_left, back_right, out_a, out_b, strip, grads,
):
    a = scal[0]
    b = scal[1]
    first, last = row_end(scal)
    n_low = low_pairs(b)
    tokens = 8 * 32

    def block_of(dim, shape):
        row = lax.broadcasted_iota(jnp.int32, shape, dim) & 31
        return (row + WIN - a) >> 3

    mask = block_of(0, (2 * tokens, tokens)) == block_of(1, (2 * tokens, tokens))

    def per_pair(p, carry):
        low = p < n_low

        def place(col):
            here = jnp.logical_xor(low, col < b)
            there = jnp.logical_not(here)
            on_right = jnp.logical_and(there, low)
            on_left = jnp.logical_and(there, jnp.logical_not(low))
            return here, on_left, on_right, p * b + col, (p - n_low) * (8 - b) + col - b

        def fetch(col, inner):
            here, on_left, on_right, slot_right, slot_left = place(col)

            def put(r, block):
                strip[r, col] = block

            @pl.when(here)
            def _():
                for r in range(4):
                    strip[r, col] = whole[r, p, col]

            @pl.when(on_right)
            def _():
                load_block(slot_right, 4, put, from_right, in_a, in_b, last)

            @pl.when(on_left)
            def _():
                load_block(slot_left, 4, put, from_left, in_a, in_b, first)

            return inner

        lax.fori_loop(0, 8, fetch, 0)
        q, k, v, g = (strip[r].reshape(tokens, LANES) for r in range(4))
        for r, grad in enumerate(attend(q, k, v, g, mask)):
            grads[r] = grad.astype(BF16).reshape(8, 32, LANES)

        def store(col, inner):
            here, on_left, on_right, slot_right, slot_left = place(col)
            block = lambda r: grads[r, col]

            @pl.when(here)
            def _():
                for r in range(3):
                    local[r, p, col] = grads[r, col]

            @pl.when(on_right)
            def _():
                store_block(slot_right, 3, block, back_right, out_a, out_b, last)

            @pl.when(on_left)
            def _():
                store_block(slot_left, 3, block, back_left, out_a, out_b, first)

            return inner

        lax.fori_loop(0, 8, store, 0)
        return carry

    lax.fori_loop(0, PAIRS, per_pair, 0)


def gather_body(scal, local, from_left, from_right, in_a, in_b, keep, send):
    b = scal[1]
    core = scal[2]
    first, last = row_end(scal)
    n_low = low_pairs(b)
    for p in range(PAIRS):
        low = p < n_low

        def move(col, target, p=p, low=low):
            here = jnp.logical_xor(low, col < b)
            there = jnp.logical_not(here)
            spot = col & 3

            def put(r, block):
                target[r, p, spot] = block

            @pl.when(here)
            def _():
                for r in range(3):
                    target[r, p, spot] = local[r, p, col]

            @pl.when(jnp.logical_and(there, low))
            def _():
                load_block(p * b + col, 3, put, from_left, in_a, in_b, first)

            @pl.when(jnp.logical_and(there, jnp.logical_not(low)))
            def _():
                slot = (p - n_low) * (8 - b) + col - b
                load_block(slot, 3, put, from_right, in_a, in_b, last)

        for i in range(4):
            move(core * 4 + i, keep)
            move((1 - core) * 4 + i, send)


def temporal_body(steps, arrived, table, out, gates):
    frames = 8
    tokens = frames * 16
    for f in range(frames):
        gates[f] = table[pl.ds(steps[f], 1), :]

    def spot(dim, shape):
        return lax.broadcasted_iota(jnp.int32, shape, dim) & 15

    mask = spot(0, (2 * tokens, tokens)) == spot(1, (2 * tokens, tokens))
    for p in range(8):
        lanes = slice(p * LANES, (p + 1) * LANES)
        q, k, v, g = (arrived[:, 16 * r : 16 * r + 16, lanes] for r in range(4))
        g = (g.astype(F32) * gates[:, :, lanes]).astype(BF16)
        q, k, v, g = (x.reshape(tokens, LANES) for x in (q, k, v, g))
        for r, grad in enumerate(attend(q, k, v, g, mask)):
            out[:, 16 * r : 16 * r + 16, lanes] = grad.astype(BF16).reshape(frames, 16, LANES)


def final_body(scal, keep, got, times, dq, dk, dv):
    core = scal[2]
    for half in range(2):

        @pl.when(core == half)
        def _():
            for r, out in enumerate((dq, dk, dv)):
                for side, part in ((half, keep), (1 - half, got)):
                    for p in range(PAIRS):
                        lo = side * PAIRS * LANES + p * LANES
                        space = part[r, p].astype(F32).reshape(8, 16, LANES)
                        time = times[:, 16 * r : 16 * r + 16, lo : lo + LANES].astype(F32)
                        out[:, lo : lo + LANES] = (space + time).astype(BF16).reshape(128, LANES)


def exchange(to_left, to_right, cross_a, cross_b):
    devices = lax.axis_size("lon")
    chips = devices // 2

    def moves(by):
        return [
            (i, ((i // 2 + by[i // 2 % ROW]) % chips) * 2 + i % 2)
            for i in range(devices)
            if i // 2 % ROW in by
        ]

    def send(x, by):
        return lax.ppermute(x, "lon", moves(by))

    beside = send(cross_b, {3: -1, 0: 1})
    from_left = send(to_right, {0: 1, 1: 1, 2: 1})
    from_right = send(to_left, {1: -1, 2: -1, 3: -1})
    column = (lax.axis_index("lon") >> 1) & 3
    outer = jnp.logical_or(column == 0, column == 3)
    far = send(jnp.where(outer, cross_a, beside), {3: ROW, 2: ROW, 1: -ROW, 0: -ROW})
    in_a = send(far, {3: -3, 0: 3})
    in_b = send(far, {2: -2, 1: 2})
    return beside, (from_left, from_right, in_a, in_b)


def shards(queries, token_keys, values, grad_out, window_shifts, noise_steps, gate_table):
    devices = lax.axis_size("lon")

    def core_swap(x):
        return lax.ppermute(x, "lon", [(i, i ^ 1) for i in range(devices)])

    def over_frames(x):
        return lax.all_to_all(x, "tm", split_axis=0, concat_axis=0, tiled=True)

    frame = lax.axis_index("tm")
    lon = lax.axis_index("lon")
    shift = lax.dynamic_slice_in_dim(window_shifts, frame, 1, 0).reshape(2)
    place = jnp.stack([lon & 1, (lon >> 1) & 3]).astype(jnp.int32)
    scal = jnp.concatenate([shift, place])
    flat = [x.reshape(128, 1024) for x in (queries, token_keys, values, grad_out)]
    half = (4, PAIRS, 4, 32, LANES)

    def sides(count):
        side = (count, SLOTS, 32, LANES)
        return [side, side, (count, HALF, 32, LANES), (count, HALF, 32, LANES)]

    with jax.named_scope("split"):
        stacked, own, other = call(
            split_body, [(8, 64, 1024), half, half], [SMEM] + [ANY] * 4, 1 << 20, 3 << 20,
            [pltpu.VMEM((4, 128, 1024), BF16), pltpu.SemaphoreType.DMA((4,))], 60,
        )(scal, *flat)
    got = core_swap(other)
    with jax.named_scope("halo"):
        whole, *out = call(
            halo_body, [(4, PAIRS, 8, 32, LANES)] + sides(4), [SMEM] + [VMEM] * 2, 1 << 20, 3 << 20
        )(scal, own, got)
    beside, arriving = exchange(*out)
    stacked, _ = lax.optimization_barrier((stacked, beside))
    arrived = over_frames(stacked)
    with jax.named_scope("spatial"):
        local, *back = call(
            spatial_body, [(3, PAIRS, 8, 32, LANES)] + sides(3), [SMEM] + [VMEM] * 5, SPATIAL_FLOPS, 4 << 20,
            [pltpu.VMEM((4, 8, 32, LANES), BF16), pltpu.VMEM((3, 8, 32, LANES), BF16)],
        )(scal, whole, *arriving)
    beside, returned = exchange(*back)
    arrived, _ = lax.optimization_barrier((arrived, beside))
    with jax.named_scope("temporal"):
        (out_time,) = call(
            temporal_body, [(8, 48, 1024)], [SMEM, VMEM, VMEM], TEMPORAL_FLOPS, 4 << 20,
            [pltpu.VMEM((8, 1, 1024), F32)],
        )(noise_steps, arrived, gate_table)
    times = over_frames(out_time)
    with jax.named_scope("gather"):
        keep, send = call(
            gather_body, [(3, PAIRS, 4, 32, LANES)] * 2, [SMEM] + [VMEM] * 5, GATHER_FLOPS, 2 << 20
        )(scal, local, *returned)
    got_back = core_swap(send)
    with jax.named_scope("final"):
        outs = call(final_body, [(128, 1024)] * 3, [SMEM] + [VMEM] * 3, 1 << 20, 3 << 20)(
            scal, keep, got_back, times
        )
    return tuple(x.reshape(1, 4, 32, 1024) for x in outs)


def solution(mesh):
    placed = P("tm", "lon", None, None)
    return jax.shard_map(
        shards,
        mesh=mesh,
        in_specs=(placed, placed, placed, placed, P(), P(), P()),
        out_specs=(placed, placed, placed),
        check_vma=False,
    )
```

```python
import jax
import jax.numpy as jnp
from jax import lax
from jax.experimental import pallas as pl
from jax.experimental.pallas import tpu as pltpu
from jax.sharding import PartitionSpec as P

HEAD_DIM = 64
WIN = 8
LANES = 128
PAIRS = 4
SLOTS = 9
HALF = 5
ROW = 4
SCALE = HEAD_DIM**-0.5
NEG = -1e30
VMEM = pl.BlockSpec(memory_space=pltpu.VMEM)
SMEM = pl.BlockSpec(memory_space=pltpu.SMEM)
ANY = pl.BlockSpec(memory_space=pl.ANY)
SPATIAL_FLOPS = 200 << 28
TEMPORAL_FLOPS = 128 << 28
HALO_FLOPS = 1 << 28
GATHER_FLOPS = 1 << 20
BF16 = jnp.bfloat16
F32 = jnp.float32


def low_pairs(b):
    one = jnp.int32(1)
    zero = jnp.int32(0)
    return sum(jnp.where(b < top, one, zero) for top in (2, 4, 5, 7))


def call(body, outs, in_specs, flops, nbytes, scratch=(), mib=24):
    return pl.pallas_call(
        body,
        out_shape=[s if isinstance(s, jax.ShapeDtypeStruct) else jax.ShapeDtypeStruct(s, BF16) for s in outs],
        in_specs=in_specs,
        out_specs=[VMEM] * len(outs),
        scratch_shapes=list(scratch),
        compiler_params=pltpu.CompilerParams(vmem_limit_bytes=mib << 20),
        cost_estimate=pl.CostEstimate(flops=flops, bytes_accessed=nbytes, transcendentals=0),
    )


def split_body(scal, q, k, v, g, stacked, own, other, held, sems):
    core = scal[2]
    copies = [pltpu.make_async_copy(ref, held.at[r], sems.at[r]) for r, ref in enumerate((q, k, v, g))]
    for copy in copies:
        copy.start()
    for r, copy in enumerate(copies):
        copy.wait()
        for i in range(8):
            stacked[i, 16 * r : 16 * r + 16, :] = held[r, 16 * i : 16 * i + 16, :]
        for half in range(2):

            @pl.when(core == half)
            def _(r=r, half=half):
                for p in range(PAIRS):
                    lo = half * PAIRS * LANES + p * LANES
                    hi = (1 - half) * PAIRS * LANES + p * LANES
                    own[r, p] = held[r, :, lo : lo + LANES].reshape(4, 32, LANES)
                    other[r, p] = held[r, :, hi : hi + LANES].reshape(4, 32, LANES)


def row_end(scal):
    return scal[3] == 0, scal[3] == 3


def store_block(slot, count, block, side, cross_a, cross_b, crosses):
    for r in range(count):
        side[r, slot] = block(r)

    @pl.when(jnp.logical_and(crosses, slot < HALF))
    def _():
        for r in range(count):
            cross_a[r, slot] = block(r)

    @pl.when(jnp.logical_and(crosses, slot >= HALF))
    def _():
        for r in range(count):
            cross_b[r, slot - HALF] = block(r)


def load_block(slot, count, put, side, cross_a, cross_b, crosses):
    @pl.when(jnp.logical_not(crosses))
    def _():
        for r in range(count):
            put(r, side[r, slot])

    @pl.when(jnp.logical_and(crosses, slot < HALF))
    def _():
        for r in range(count):
            put(r, cross_a[r, slot])

    @pl.when(jnp.logical_and(crosses, slot >= HALF))
    def _():
        for r in range(count):
            put(r, cross_b[r, slot - HALF])


def halo_body(scal, steps, own, got, table, whole, to_left, to_right, cross_a, cross_b, gates):
    b = scal[1]
    core = scal[2]
    first, last = row_end(scal)
    n_low = low_pairs(b)
    for f in range(8):
        gates[f] = table[pl.ds(steps[f], 1), :]
    for r in range(4):
        for p in range(PAIRS):
            whole[r, p, pl.ds(core * 4, 4)] = own[r, p]
            whole[r, p, pl.ds((1 - core) * 4, 4)] = got[r, p]
    for p in range(PAIRS):

        @pl.when(p < n_low)
        def _(p=p):
            def put(col, carry):
                block = lambda r: whole[r, p, col]
                store_block(p * b + col, 4, block, to_left, cross_a, cross_b, first)
                return carry

            lax.fori_loop(0, b, put, 0)

        @pl.when(p >= n_low)
        def _(p=p):
            def put(col, carry):
                block = lambda r: whole[r, p, col]
                slot = (p - n_low) * (8 - b) + col - b
                store_block(slot, 4, block, to_right, cross_a, cross_b, last)
                return carry

            lax.fori_loop(b, 8, put, 0)


def attend(q, k, v, g, mask):
    tokens = q.shape[0]
    lane = lax.broadcasted_iota(jnp.int32, (1, LANES), 1)
    first = jnp.where(lane < HEAD_DIM, 1.0, 0.0).astype(BF16)
    second = jnp.where(lane < HEAD_DIM, 0.0, 1.0).astype(BF16)
    q = q * jnp.asarray(SCALE, BF16)
    q2 = jnp.concatenate([q * first, q * second], axis=0)
    g2 = jnp.concatenate([g * first, g * second], axis=0)
    over_last = (((1,), (1,)), ((), ()))
    over_first = (((0,), (0,)), ((), ()))
    s = lax.dot_general(q2, k, over_last, preferred_element_type=F32)
    dp = lax.dot_general(g2, v, over_last, preferred_element_type=F32)
    s = jnp.where(mask, s, NEG)
    e = jnp.exp(s - jnp.max(s, axis=1, keepdims=True))
    p = e * (1.0 / jnp.sum(e, axis=1, keepdims=True))
    delta = jnp.sum(p * dp, axis=1, keepdims=True)
    ds = (p * (dp - delta)).astype(BF16)
    p = p.astype(BF16)
    dv = lax.dot_general(p, g2, over_first, preferred_element_type=F32)
    dk = lax.dot_general(ds, q2, over_first, preferred_element_type=F32)
    dq = jnp.dot(ds[:tokens], k * first, preferred_element_type=F32)
    dq = dq + jnp.dot(ds[tokens:], k * second, preferred_element_type=F32)
    return (dq * SCALE, dk, dv)


def spatial_body(
    scal, whole, from_left, from_right, in_a, in_b,
    local, back_left, back_right, out_a, out_b, strip, grads,
):
    a = scal[0]
    b = scal[1]
    first, last = row_end(scal)
    n_low = low_pairs(b)
    tokens = 8 * 32

    def block_of(dim, shape):
        row = lax.broadcasted_iota(jnp.int32, shape, dim) & 31
        return (row + WIN - a) >> 3

    mask = block_of(0, (2 * tokens, tokens)) == block_of(1, (2 * tokens, tokens))

    def per_pair(p, carry):
        low = p < n_low

        def place(col):
            here = jnp.logical_xor(low, col < b)
            there = jnp.logical_not(here)
            on_right = jnp.logical_and(there, low)
            on_left = jnp.logical_and(there, jnp.logical_not(low))
            return here, on_left, on_right, p * b + col, (p - n_low) * (8 - b) + col - b

        def fetch(col, inner):
            here, on_left, on_right, slot_right, slot_left = place(col)

            def put(r, block):
                strip[r, col] = block

            @pl.when(here)
            def _():
                for r in range(4):
                    strip[r, col] = whole[r, p, col]

            @pl.when(on_right)
            def _():
                load_block(slot_right, 4, put, from_right, in_a, in_b, last)

            @pl.when(on_left)
            def _():
                load_block(slot_left, 4, put, from_left, in_a, in_b, first)

            return inner

        lax.fori_loop(0, 8, fetch, 0)
        q, k, v, g = (strip[r].reshape(tokens, LANES) for r in range(4))
        for r, grad in enumerate(attend(q, k, v, g, mask)):
            grads[r] = grad.astype(BF16).reshape(8, 32, LANES)

        def store(col, inner):
            here, on_left, on_right, slot_right, slot_left = place(col)
            block = lambda r: grads[r, col]

            @pl.when(here)
            def _():
                for r in range(3):
                    local[r, p, col] = grads[r, col]

            @pl.when(on_right)
            def _():
                store_block(slot_right, 3, block, back_right, out_a, out_b, last)

            @pl.when(on_left)
            def _():
                store_block(slot_left, 3, block, back_left, out_a, out_b, first)

            return inner

        lax.fori_loop(0, 8, store, 0)
        return carry

    lax.fori_loop(0, PAIRS, per_pair, 0)


def gather_body(scal, local, from_left, from_right, in_a, in_b, keep, send):
    b = scal[1]
    core = scal[2]
    first, last = row_end(scal)
    n_low = low_pairs(b)
    for p in range(PAIRS):
        low = p < n_low

        def move(col, target, p=p, low=low):
            here = jnp.logical_xor(low, col < b)
            there = jnp.logical_not(here)
            spot = col & 3

            def put(r, block):
                target[r, p, spot] = block

            @pl.when(here)
            def _():
                for r in range(3):
                    target[r, p, spot] = local[r, p, col]

            @pl.when(jnp.logical_and(there, low))
            def _():
                load_block(p * b + col, 3, put, from_left, in_a, in_b, first)

            @pl.when(jnp.logical_and(there, jnp.logical_not(low)))
            def _():
                slot = (p - n_low) * (8 - b) + col - b
                load_block(slot, 3, put, from_right, in_a, in_b, last)

        for i in range(4):
            move(core * 4 + i, keep)
            move((1 - core) * 4 + i, send)


def temporal_body(arrived, gates, out):
    frames = 8
    tokens = frames * 16

    def spot(dim, shape):
        return lax.broadcasted_iota(jnp.int32, shape, dim) & 15

    mask = spot(0, (2 * tokens, tokens)) == spot(1, (2 * tokens, tokens))
    for p in range(8):
        lanes = slice(p * LANES, (p + 1) * LANES)
        q, k, v, g = (arrived[:, 16 * r : 16 * r + 16, lanes] for r in range(4))
        g = (g.astype(F32) * gates[:, :, lanes]).astype(BF16)
        q, k, v, g = (x.reshape(tokens, LANES) for x in (q, k, v, g))
        for r, grad in enumerate(attend(q, k, v, g, mask)):
            out[:, 16 * r : 16 * r + 16, lanes] = grad.astype(BF16).reshape(frames, 16, LANES)


def final_body(scal, keep, got, times, dq, dk, dv):
    core = scal[2]
    for half in range(2):

        @pl.when(core == half)
        def _():
            for r, out in enumerate((dq, dk, dv)):
                for side, part in ((half, keep), (1 - half, got)):
                    for p in range(PAIRS):
                        lo = side * PAIRS * LANES + p * LANES
                        space = part[r, p].astype(F32).reshape(8, 16, LANES)
                        time = times[:, 16 * r : 16 * r + 16, lo : lo + LANES].astype(F32)
                        out[:, lo : lo + LANES] = (space + time).astype(BF16).reshape(128, LANES)


def exchange(to_left, to_right, cross_a, cross_b, late=False):
    devices = lax.axis_size("lon")
    chips = devices // 2

    def moves(by):
        return [
            (i, ((i // 2 + by[i // 2 % ROW]) % chips) * 2 + i % 2)
            for i in range(devices)
            if i // 2 % ROW in by
        ]

    def send(x, by):
        return lax.ppermute(x, "lon", moves(by))

    beside = send(cross_b, {3: -1, 0: 1})
    if late:
        to_left, to_right, beside = lax.optimization_barrier((to_left, to_right, beside))
    from_left = send(to_right, {0: 1, 1: 1, 2: 1})
    from_right = send(to_left, {1: -1, 2: -1, 3: -1})
    if late:
        cross_a, beside, from_left, from_right = lax.optimization_barrier(
            (cross_a, beside, from_left, from_right)
        )
    in_a = send(cross_a, {3: 1, 0: -1})
    in_b = send(beside, {2: 2, 1: -2})
    return beside, (from_left, from_right, in_a, in_b)


def shards(queries, token_keys, values, grad_out, window_shifts, noise_steps, gate_table):
    devices = lax.axis_size("lon")

    def core_swap(x):
        return lax.ppermute(x, "lon", [(i, i ^ 1) for i in range(devices)])

    def over_frames(x):
        return lax.all_to_all(x, "tm", split_axis=0, concat_axis=0, tiled=True)

    frame = lax.axis_index("tm")
    lon = lax.axis_index("lon")
    shift = lax.dynamic_slice_in_dim(window_shifts, frame, 1, 0).reshape(2)
    place = jnp.stack([lon & 1, (lon >> 1) & 3]).astype(jnp.int32)
    scal = jnp.concatenate([shift, place])
    flat = [x.reshape(128, 1024) for x in (queries, token_keys, values, grad_out)]
    half = (4, PAIRS, 4, 32, LANES)

    def sides(count):
        side = (count, SLOTS, 32, LANES)
        return [side, side, (count, HALF, 32, LANES), (count, SLOTS - HALF, 32, LANES)]

    with jax.named_scope("split"):
        stacked, own, other = call(
            split_body, [(8, 64, 1024), half, half], [SMEM] + [ANY] * 4, 1 << 20, 3 << 20,
            [pltpu.VMEM((4, 128, 1024), BF16), pltpu.SemaphoreType.DMA((4,))], 60,
        )(scal, *flat)
    arrived = over_frames(stacked)
    got = core_swap(other)
    with jax.named_scope("halo"):
        whole, *out, gates = call(
            halo_body, [(4, PAIRS, 8, 32, LANES)] + sides(4) + [jax.ShapeDtypeStruct((8, 1, 1024), F32)],
            [SMEM] * 2 + [VMEM] * 3, HALO_FLOPS, 3 << 20,
        )(scal, noise_steps, own, got, gate_table)
    beside, arriving = exchange(*out, late=True)
    arrived, _ = lax.optimization_barrier((arrived, beside))
    with jax.named_scope("temporal"):
        (out_time,) = call(
            temporal_body, [(8, 48, 1024)], [VMEM, VMEM], TEMPORAL_FLOPS, 4 << 20
        )(arrived, gates)
    times = over_frames(out_time)
    with jax.named_scope("spatial"):
        local, *back = call(
            spatial_body, [(3, PAIRS, 8, 32, LANES)] + sides(3), [SMEM] + [VMEM] * 5, SPATIAL_FLOPS, 4 << 20,
            [pltpu.VMEM((4, 8, 32, LANES), BF16), pltpu.VMEM((3, 8, 32, LANES), BF16)],
        )(scal, whole, *arriving)
    _, returned = exchange(*back)
    with jax.named_scope("gather"):
        keep, send = call(
            gather_body, [(3, PAIRS, 4, 32, LANES)] * 2, [SMEM] + [VMEM] * 5, GATHER_FLOPS, 2 << 20
        )(scal, local, *returned)
    got_back = core_swap(send)
    with jax.named_scope("final"):
        outs = call(final_body, [(128, 1024)] * 3, [SMEM] + [VMEM] * 3, 1 << 20, 3 << 20)(
            scal, keep, got_back, times
        )
    return tuple(x.reshape(1, 4, 32, 1024) for x in outs)


def solution(mesh):
    placed = P("tm", "lon", None, None)
    return jax.shard_map(
        shards,
        mesh=mesh,
        in_specs=(placed, placed, placed, placed, P(), P(), P()),
        out_specs=(placed, placed, placed),
        check_vma=False,
    )
```

```python
import jax
import jax.numpy as jnp
from jax import lax
from jax.experimental import pallas as pl
from jax.experimental.pallas import tpu as pltpu
from jax.sharding import PartitionSpec as P

HEAD_DIM = 64
WIN = 8
LANES = 128
PAIRS = 4
SLOTS = 9
HALF = 5
ROW = 4
SCALE = HEAD_DIM**-0.5
NEG = -1e30
VMEM = pl.BlockSpec(memory_space=pltpu.VMEM)
SMEM = pl.BlockSpec(memory_space=pltpu.SMEM)
ANY = pl.BlockSpec(memory_space=pl.ANY)
SPATIAL_FLOPS = 200 << 28
TEMPORAL_FLOPS = 128 << 28
HALO_FLOPS = 1 << 28
SIDES_FLOPS = 1 << 20
GATHER_FLOPS = 1 << 20
BF16 = jnp.bfloat16
F32 = jnp.float32


def low_pairs(b):
    one = jnp.int32(1)
    zero = jnp.int32(0)
    return sum(jnp.where(b < top, one, zero) for top in (2, 4, 5, 7))


def call(body, outs, in_specs, flops, nbytes, scratch=(), mib=24):
    return pl.pallas_call(
        body,
        out_shape=[s if isinstance(s, jax.ShapeDtypeStruct) else jax.ShapeDtypeStruct(s, BF16) for s in outs],
        in_specs=in_specs,
        out_specs=[VMEM] * len(outs),
        scratch_shapes=list(scratch),
        compiler_params=pltpu.CompilerParams(vmem_limit_bytes=mib << 20),
        cost_estimate=pl.CostEstimate(flops=flops, bytes_accessed=nbytes, transcendentals=0),
    )


def split_body(q, k, v, g, stacked, own, other, sems):
    core = lax.axis_index("lon") & 1
    copies = [
        [
            pltpu.make_async_copy(
                ref.at[pl.ds(16 * i, 16)], stacked.at[i, pl.ds(16 * r, 16)], sems.at[r, i]
            )
            for i in range(8)
        ]
        for r, ref in enumerate((q, k, v, g))
    ]
    for row in copies:
        for copy in row:
            copy.start()
    for r, row in enumerate(copies):
        for copy in row:
            copy.wait()
        for half in range(2):

            @pl.when(core == half)
            def _(r=r, half=half):
                for p in range(PAIRS):
                    lo = half * PAIRS * LANES + p * LANES
                    hi = (1 - half) * PAIRS * LANES + p * LANES
                    rows = slice(16 * r, 16 * r + 16)
                    own[r, p] = stacked[:, rows, lo : lo + LANES].reshape(4, 32, LANES)
                    other[r, p] = stacked[:, rows, hi : hi + LANES].reshape(4, 32, LANES)


def row_end(scal):
    return scal[3] == 0, scal[3] == 3


def store_cross(slot, count, block, cross_a, cross_b, crosses):
    @pl.when(jnp.logical_and(crosses, slot < HALF))
    def _():
        for r in range(count):
            cross_a[r, slot] = block(r)

    @pl.when(jnp.logical_and(crosses, slot >= HALF))
    def _():
        for r in range(count):
            cross_b[r, slot - HALF] = block(r)


def load_block(slot, count, put, side, cross_a, cross_b, crosses):
    @pl.when(jnp.logical_not(crosses))
    def _():
        for r in range(count):
            put(r, side[r, slot])

    @pl.when(jnp.logical_and(crosses, slot < HALF))
    def _():
        for r in range(count):
            put(r, cross_a[r, slot])

    @pl.when(jnp.logical_and(crosses, slot >= HALF))
    def _():
        for r in range(count):
            put(r, cross_b[r, slot - HALF])


def halo_body(scal, steps, own, got, table, whole, to_left, to_right, cross_a, cross_b, gates):
    b = scal[1]
    core = scal[2]
    first, last = row_end(scal)
    n_low = low_pairs(b)
    for f in range(8):
        gates[f] = table[pl.ds(steps[f], 1), :]
    for r in range(4):
        for p in range(PAIRS):
            whole[r, p, pl.ds(core * 4, 4)] = own[r, p]
            whole[r, p, pl.ds((1 - core) * 4, 4)] = got[r, p]
    for p in range(PAIRS):

        @pl.when(p < n_low)
        def _(p=p):
            def put(col, carry):
                for r in range(4):
                    to_left[r, p * b + col] = whole[r, p, col]
                store_cross(p * b + col, 4, lambda r: whole[r, p, col], cross_a, cross_b, first)
                return carry

            lax.fori_loop(0, b, put, 0)

        @pl.when(p >= n_low)
        def _(p=p):
            def put(col, carry):
                slot = (p - n_low) * (8 - b) + col - b
                for r in range(4):
                    to_right[r, slot] = whole[r, p, col]
                store_cross(slot, 4, lambda r: whole[r, p, col], cross_a, cross_b, last)
                return carry

            lax.fori_loop(b, 8, put, 0)


def attend(q, k, v, g, mask):
    tokens = q.shape[0]
    lane = lax.broadcasted_iota(jnp.int32, (1, LANES), 1)
    first = jnp.where(lane < HEAD_DIM, 1.0, 0.0).astype(BF16)
    second = jnp.where(lane < HEAD_DIM, 0.0, 1.0).astype(BF16)
    q = q * jnp.asarray(SCALE, BF16)
    q2 = jnp.concatenate([q * first, q * second], axis=0)
    g2 = jnp.concatenate([g * first, g * second], axis=0)
    over_last = (((1,), (1,)), ((), ()))
    over_first = (((0,), (0,)), ((), ()))
    s = lax.dot_general(k, q2, over_last, preferred_element_type=F32)
    dp = lax.dot_general(v, g2, over_last, preferred_element_type=F32)
    s = jnp.where(mask, s, NEG)
    e = jnp.exp(s - jnp.max(s, axis=0, keepdims=True))
    p = e * (1.0 / jnp.sum(e, axis=0, keepdims=True))
    delta = jnp.sum(p * dp, axis=0, keepdims=True)
    ds = (p * (dp - delta)).astype(BF16)
    p = p.astype(BF16)
    dv = jnp.dot(p, g2, preferred_element_type=F32)
    dk = jnp.dot(ds, q2, preferred_element_type=F32)
    dq = lax.dot_general(ds[:, :tokens], k * first, over_first, preferred_element_type=F32)
    dq = dq + lax.dot_general(ds[:, tokens:], k * second, over_first, preferred_element_type=F32)
    return (dq * SCALE, dk, dv)


def spatial_body(scal, whole, from_left, from_right, in_a, in_b, strips, out_a, out_b, strip):
    a = scal[0]
    b = scal[1]
    first, last = row_end(scal)
    n_low = low_pairs(b)
    tokens = 8 * 32

    def block_of(dim, shape):
        row = lax.broadcasted_iota(jnp.int32, shape, dim) & 31
        return (row + WIN - a) >> 3

    mask = block_of(0, (tokens, 2 * tokens)) == block_of(1, (tokens, 2 * tokens))

    for p in range(PAIRS):
        low = p < n_low

        def slot_of(col, p=p):
            return p * b + col, (p - n_low) * (8 - b) + col - b

        @pl.when(low)
        def _(p=p):
            def here(col, carry):
                for r in range(4):
                    strip[p, r, col] = whole[r, p, col]
                return carry

            def there(col, carry):
                def put(r, block):
                    strip[p, r, col] = block

                load_block(slot_of(col)[0], 4, put, from_right, in_a, in_b, last)
                return carry

            lax.fori_loop(b, 8, here, 0)
            lax.fori_loop(0, b, there, 0)

        @pl.when(jnp.logical_not(low))
        def _(p=p):
            def here(col, carry):
                for r in range(4):
                    strip[p, r, col] = whole[r, p, col]
                return carry

            def there(col, carry):
                def put(r, block):
                    strip[p, r, col] = block

                load_block(slot_of(col)[1], 4, put, from_left, in_a, in_b, first)
                return carry

            lax.fori_loop(0, b, here, 0)
            lax.fori_loop(b, 8, there, 0)

    for p in range(PAIRS):
        q, k, v, g = (strip[p, r].reshape(tokens, LANES) for r in range(4))
        for r, grad in enumerate(attend(q, k, v, g, mask)):
            strips[r, p] = grad.astype(BF16).reshape(8, 32, LANES)

    for p in range(PAIRS):
        low = p < n_low

        def out(col, carry, p=p, low=low):
            block = lambda r: strips[r, p, col]
            slot = jnp.where(low, p * b + col, (p - n_low) * (8 - b) + col - b)
            store_cross(slot, 3, block, out_a, out_b, jnp.where(low, scal[3], 3 - scal[3]) == 3)
            return carry

        lax.fori_loop(jnp.where(low, 0, b), jnp.where(low, b, 8), out, 0)


def sides_body(scal, strips, back_left, back_right):
    b = scal[1]
    n_low = low_pairs(b)
    for p in range(PAIRS):

        @pl.when(p < n_low)
        def _(p=p):
            def put(col, carry):
                for r in range(3):
                    back_right[r, p * b + col] = strips[r, p, col]
                return carry

            lax.fori_loop(0, b, put, 0)

        @pl.when(p >= n_low)
        def _(p=p):
            def put(col, carry):
                for r in range(3):
                    back_left[r, (p - n_low) * (8 - b) + col - b] = strips[r, p, col]
                return carry

            lax.fori_loop(b, 8, put, 0)


def gather_body(scal, local, from_left, from_right, in_a, in_b, keep, send):
    b = scal[1]
    core = scal[2]
    first, last = row_end(scal)
    n_low = low_pairs(b)
    for p in range(PAIRS):
        low = p < n_low

        def move(col, target, p=p, low=low):
            here = jnp.logical_xor(low, col < b)
            there = jnp.logical_not(here)
            spot = col & 3

            def put(r, block):
                target[r, p, spot] = block

            @pl.when(here)
            def _():
                for r in range(3):
                    target[r, p, spot] = local[r, p, col]

            @pl.when(jnp.logical_and(there, low))
            def _():
                load_block(p * b + col, 3, put, from_left, in_a, in_b, first)

            @pl.when(jnp.logical_and(there, jnp.logical_not(low)))
            def _():
                slot = (p - n_low) * (8 - b) + col - b
                load_block(slot, 3, put, from_right, in_a, in_b, last)

        for i in range(4):
            move(core * 4 + i, keep)
            move((1 - core) * 4 + i, send)


def temporal_body(arrived, gates, out):
    frames = 8
    tokens = frames * 16

    def spot(dim, shape):
        return lax.broadcasted_iota(jnp.int32, shape, dim) & 15

    mask = spot(0, (tokens, 2 * tokens)) == spot(1, (tokens, 2 * tokens))
    for p in range(8):
        lanes = slice(p * LANES, (p + 1) * LANES)
        q, k, v, g = (arrived[:, 16 * r : 16 * r + 16, lanes] for r in range(4))
        g = (g.astype(F32) * gates[:, :, lanes]).astype(BF16)
        q, k, v, g = (x.reshape(tokens, LANES) for x in (q, k, v, g))
        for r, grad in enumerate(attend(q, k, v, g, mask)):
            out[:, 16 * r : 16 * r + 16, lanes] = grad.astype(BF16).reshape(frames, 16, LANES)


def final_body(scal, keep, got, times, dq, dk, dv):
    core = scal[2]
    for half in range(2):

        @pl.when(core == half)
        def _():
            for r, out in enumerate((dq, dk, dv)):
                for side, part in ((half, keep), (1 - half, got)):
                    for p in range(PAIRS):
                        lo = side * PAIRS * LANES + p * LANES
                        space = part[r, p].astype(F32).reshape(8, 16, LANES)
                        time = times[:, 16 * r : 16 * r + 16, lo : lo + LANES].astype(F32)
                        out[:, lo : lo + LANES] = (space + time).astype(BF16).reshape(128, LANES)


def send(x, by):
    devices = lax.axis_size("lon")
    chips = devices // 2
    moves = [
        (i, ((i // 2 + by[i // 2 % ROW]) % chips) * 2 + i % 2) for i in range(devices) if i // 2 % ROW in by
    ]
    return lax.ppermute(x, "lon", moves)


def scatter_row(cross_b):
    return send(cross_b, {3: -1, 0: 1})


def cross_rows(cross_a, beside):
    return send(cross_a, {3: 1, 0: -1}), send(beside, {2: 2, 1: -2})


def in_row(to_left, to_right):
    return send(to_right, {0: 1, 1: 1, 2: 1}), send(to_left, {1: -1, 2: -1, 3: -1})


def shards(queries, token_keys, values, grad_out, window_shifts, noise_steps, gate_table):
    devices = lax.axis_size("lon")

    def core_swap(x):
        return lax.ppermute(x, "lon", [(i, i ^ 1) for i in range(devices)])

    def over_frames(x):
        return lax.all_to_all(x, "tm", split_axis=0, concat_axis=0, tiled=True)

    frame = lax.axis_index("tm")
    lon = lax.axis_index("lon")
    shift = lax.dynamic_slice_in_dim(window_shifts, frame, 1, 0).reshape(2)
    place = jnp.stack([lon & 1, (lon >> 1) & 3]).astype(jnp.int32)
    scal = jnp.concatenate([shift, place])
    flat = [x.reshape(128, 1024) for x in (queries, token_keys, values, grad_out)]
    half = (4, PAIRS, 4, 32, LANES)

    def sides(count):
        side = (count, SLOTS, 32, LANES)
        return [side, side, (count, HALF, 32, LANES), (count, SLOTS - HALF, 32, LANES)]

    with jax.named_scope("split"):
        stacked, own, other = call(
            split_body, [(8, 64, 1024), half, half], [ANY] * 4, 1 << 20, 3 << 20,
            [pltpu.SemaphoreType.DMA((4, 8))], 60,
        )(*flat)
    arrived = over_frames(stacked)
    got = core_swap(other)
    with jax.named_scope("halo"):
        whole, *out, gates = call(
            halo_body, [(4, PAIRS, 8, 32, LANES)] + sides(4) + [jax.ShapeDtypeStruct((8, 1, 1024), F32)],
            [SMEM] * 2 + [VMEM] * 3, HALO_FLOPS, 3 << 20,
        )(scal, noise_steps, own, got, gate_table)
    to_left, to_right, cross_a, cross_b = out
    beside = scatter_row(cross_b)
    to_left, to_right, beside = lax.optimization_barrier((to_left, to_right, beside))
    from_left, from_right = in_row(to_left, to_right)
    cross_a, beside, from_left, from_right = lax.optimization_barrier((cross_a, beside, from_left, from_right))
    in_a, in_b = cross_rows(cross_a, beside)
    arrived, _ = lax.optimization_barrier((arrived, beside))
    with jax.named_scope("temporal"):
        (out_time,) = call(
            temporal_body, [(8, 48, 1024)], [VMEM, VMEM], TEMPORAL_FLOPS, 4 << 20
        )(arrived, gates)
    times = over_frames(out_time)
    with jax.named_scope("spatial"):
        strips, out_a, out_b = call(
            spatial_body, [(3, PAIRS, 8, 32, LANES)] + sides(3)[2:], [SMEM] + [VMEM] * 5, SPATIAL_FLOPS, 4 << 20,
            [pltpu.VMEM((PAIRS, 4, 8, 32, LANES), BF16)],
        )(scal, whole, from_left, from_right, in_a, in_b)
    beside = scatter_row(out_b)
    out_a, beside = lax.optimization_barrier((out_a, beside))
    in_a, in_b = cross_rows(out_a, beside)
    with jax.named_scope("sides"):
        back_left, back_right = call(sides_body, sides(3)[:2], [SMEM, VMEM], SIDES_FLOPS, 1 << 20)(scal, strips)
    from_left, from_right = in_row(back_left, back_right)
    with jax.named_scope("gather"):
        keep, send = call(
            gather_body, [(3, PAIRS, 4, 32, LANES)] * 2, [SMEM] + [VMEM] * 5, GATHER_FLOPS, 2 << 20
        )(scal, strips, from_left, from_right, in_a, in_b)
    got_back = core_swap(send)
    with jax.named_scope("final"):
        outs = call(final_body, [(128, 1024)] * 3, [SMEM] + [VMEM] * 3, 1 << 20, 3 << 20)(
            scal, keep, got_back, times
        )
    return tuple(x.reshape(1, 4, 32, 1024) for x in outs)


def solution(mesh):
    placed = P("tm", "lon", None, None)
    return jax.shard_map(
        shards,
        mesh=mesh,
        in_specs=(placed, placed, placed, placed, P(), P(), P()),
        out_specs=(placed, placed, placed),
        check_vma=False,
    )
```

```python
import jax
import jax.numpy as jnp
from jax import lax
from jax.experimental import pallas as pl
from jax.experimental.pallas import tpu as pltpu
from jax.sharding import PartitionSpec as P

HEAD_DIM = 64
WIN = 8
LANES = 128
PAIRS = 4
SLOTS = 9
HALF = 5
ROW = 4
SCALE = HEAD_DIM**-0.5
NEG = -1e30
VMEM = pl.BlockSpec(memory_space=pltpu.VMEM)
SMEM = pl.BlockSpec(memory_space=pltpu.SMEM)
ANY = pl.BlockSpec(memory_space=pl.ANY)
SPATIAL_FLOPS = 200 << 28
TEMPORAL_FLOPS = 128 << 28
HALO_FLOPS = 1 << 28
SIDES_FLOPS = 1 << 20
GATHER_FLOPS = 1 << 20
BF16 = jnp.bfloat16
F32 = jnp.float32


def low_pairs(b):
    one = jnp.int32(1)
    zero = jnp.int32(0)
    return sum(jnp.where(b < top, one, zero) for top in (2, 4, 5, 7))


def call(body, outs, in_specs, flops, nbytes, scratch=(), mib=24):
    return pl.pallas_call(
        body,
        out_shape=[s if isinstance(s, jax.ShapeDtypeStruct) else jax.ShapeDtypeStruct(s, BF16) for s in outs],
        in_specs=in_specs,
        out_specs=[VMEM] * len(outs),
        scratch_shapes=list(scratch),
        compiler_params=pltpu.CompilerParams(vmem_limit_bytes=mib << 20),
        cost_estimate=pl.CostEstimate(flops=flops, bytes_accessed=nbytes, transcendentals=0),
    )


def split_body(q, k, v, g, stacked, own, other, sems):
    core = lax.axis_index("lon") & 1
    copies = [
        [
            pltpu.make_async_copy(
                ref.at[pl.ds(16 * i, 16)], stacked.at[i, pl.ds(16 * r, 16)], sems.at[r, i]
            )
            for i in range(8)
        ]
        for r, ref in enumerate((q, k, v, g))
    ]
    for row in copies:
        for copy in row:
            copy.start()
    for r, row in enumerate(copies):
        for copy in row:
            copy.wait()
        for half in range(2):

            @pl.when(core == half)
            def _(r=r, half=half):
                for p in range(PAIRS):
                    lo = half * PAIRS * LANES + p * LANES
                    hi = (1 - half) * PAIRS * LANES + p * LANES
                    rows = slice(16 * r, 16 * r + 16)
                    own[r, p] = stacked[:, rows, lo : lo + LANES].reshape(4, 32, LANES)
                    other[r, p] = stacked[:, rows, hi : hi + LANES].reshape(4, 32, LANES)


def row_end(scal):
    return scal[3] == 0, scal[3] == 3


def store_cross(slot, count, block, cross_a, cross_b, crosses):
    @pl.when(jnp.logical_and(crosses, slot < HALF))
    def _():
        for r in range(count):
            cross_a[r, slot] = block(r)

    @pl.when(jnp.logical_and(crosses, slot >= HALF))
    def _():
        for r in range(count):
            cross_b[r, slot - HALF] = block(r)


def load_block(slot, count, put, side, cross_a, cross_b, crosses):
    @pl.when(jnp.logical_not(crosses))
    def _():
        for r in range(count):
            put(r, side[r, slot])

    @pl.when(jnp.logical_and(crosses, slot < HALF))
    def _():
        for r in range(count):
            put(r, cross_a[r, slot])

    @pl.when(jnp.logical_and(crosses, slot >= HALF))
    def _():
        for r in range(count):
            put(r, cross_b[r, slot - HALF])


def halo_body(scal, steps, own, got, table, whole, to_left, to_right, cross_a, cross_b, gates):
    b = scal[1]
    core = scal[2]
    first, last = row_end(scal)
    n_low = low_pairs(b)
    for f in range(8):
        gates[f] = table[pl.ds(steps[f], 1), :]
    for r in range(4):
        for p in range(PAIRS):
            whole[r, p, pl.ds(core * 4, 4)] = own[r, p]
            whole[r, p, pl.ds((1 - core) * 4, 4)] = got[r, p]
    for p in range(PAIRS):

        @pl.when(p < n_low)
        def _(p=p):
            def put(col, carry):
                for r in range(4):
                    to_left[r, p * b + col] = whole[r, p, col]
                store_cross(p * b + col, 4, lambda r: whole[r, p, col], cross_a, cross_b, first)
                return carry

            lax.fori_loop(0, b, put, 0)

        @pl.when(p >= n_low)
        def _(p=p):
            def put(col, carry):
                slot = (p - n_low) * (8 - b) + col - b
                for r in range(4):
                    to_right[r, slot] = whole[r, p, col]
                store_cross(slot, 4, lambda r: whole[r, p, col], cross_a, cross_b, last)
                return carry

            lax.fori_loop(b, 8, put, 0)


def attend(q, k, v, g, mask):
    tokens = q.shape[0]
    lane = lax.broadcasted_iota(jnp.int32, (1, LANES), 1)
    first = jnp.where(lane < HEAD_DIM, 1.0, 0.0).astype(BF16)
    second = jnp.where(lane < HEAD_DIM, 0.0, 1.0).astype(BF16)
    q = q * jnp.asarray(SCALE, BF16)
    q2 = jnp.concatenate([q * first, q * second], axis=0)
    g2 = jnp.concatenate([g * first, g * second], axis=0)
    over_last = (((1,), (1,)), ((), ()))
    over_first = (((0,), (0,)), ((), ()))
    s = lax.dot_general(k, q2, over_last, preferred_element_type=F32)
    dp = lax.dot_general(v, g2, over_last, preferred_element_type=F32)
    s = jnp.where(mask, s, NEG)
    e = jnp.exp(s - jnp.max(s, axis=0, keepdims=True))
    p = e * (1.0 / jnp.sum(e, axis=0, keepdims=True))
    delta = jnp.sum(p * dp, axis=0, keepdims=True)
    ds = (p * (dp - delta)).astype(BF16)
    p = p.astype(BF16)
    dv = jnp.dot(p, g2, preferred_element_type=F32)
    dk = jnp.dot(ds, q2, preferred_element_type=F32)
    dq = lax.dot_general(ds[:, :tokens], k * first, over_first, preferred_element_type=F32)
    dq = dq + lax.dot_general(ds[:, tokens:], k * second, over_first, preferred_element_type=F32)
    return (dq * SCALE, dk, dv)


def spatial_body(scal, whole, from_left, from_right, in_a, in_b, strips, out_a, out_b, strip):
    a = scal[0]
    b = scal[1]
    first, last = row_end(scal)
    n_low = low_pairs(b)
    tokens = 8 * 32

    def block_of(dim, shape):
        row = lax.broadcasted_iota(jnp.int32, shape, dim) & 31
        return (row + WIN - a) >> 3

    mask = block_of(0, (tokens, 2 * tokens)) == block_of(1, (tokens, 2 * tokens))

    for p in range(PAIRS):
        low = p < n_low

        def slot_of(col, p=p):
            return p * b + col, (p - n_low) * (8 - b) + col - b

        @pl.when(low)
        def _(p=p):
            def here(col, carry):
                for r in range(4):
                    strip[p, r, col] = whole[r, p, col]
                return carry

            def there(col, carry):
                def put(r, block):
                    strip[p, r, col] = block

                load_block(slot_of(col)[0], 4, put, from_right, in_a, in_b, last)
                return carry

            lax.fori_loop(b, 8, here, 0)
            lax.fori_loop(0, b, there, 0)

        @pl.when(jnp.logical_not(low))
        def _(p=p):
            def here(col, carry):
                for r in range(4):
                    strip[p, r, col] = whole[r, p, col]
                return carry

            def there(col, carry):
                def put(r, block):
                    strip[p, r, col] = block

                load_block(slot_of(col)[1], 4, put, from_left, in_a, in_b, first)
                return carry

            lax.fori_loop(0, b, here, 0)
            lax.fori_loop(b, 8, there, 0)

    for p in range(PAIRS):
        q, k, v, g = (strip[p, r].reshape(tokens, LANES) for r in range(4))
        for r, grad in enumerate(attend(q, k, v, g, mask)):
            strips[r, p] = grad.astype(BF16).reshape(8, 32, LANES)

    for p in range(PAIRS):
        low = p < n_low

        def out(col, carry, p=p, low=low):
            block = lambda r: strips[r, p, col]
            slot = jnp.where(low, p * b + col, (p - n_low) * (8 - b) + col - b)
            store_cross(slot, 3, block, out_a, out_b, jnp.where(low, scal[3], 3 - scal[3]) == 3)
            return carry

        lax.fori_loop(jnp.where(low, 0, b), jnp.where(low, b, 8), out, 0)


def sides_body(scal, strips, back_left, back_right):
    b = scal[1]
    n_low = low_pairs(b)
    for p in range(PAIRS):

        @pl.when(p < n_low)
        def _(p=p):
            def put(col, carry):
                for r in range(3):
                    back_right[r, p * b + col] = strips[r, p, col]
                return carry

            lax.fori_loop(0, b, put, 0)

        @pl.when(p >= n_low)
        def _(p=p):
            def put(col, carry):
                for r in range(3):
                    back_left[r, (p - n_low) * (8 - b) + col - b] = strips[r, p, col]
                return carry

            lax.fori_loop(b, 8, put, 0)


def gather_body(scal, local, from_left, from_right, in_a, in_b, keep, send):
    b = scal[1]
    core = scal[2]
    first, last = row_end(scal)
    n_low = low_pairs(b)
    for p in range(PAIRS):
        low = p < n_low

        def move(col, target, p=p, low=low):
            here = jnp.logical_xor(low, col < b)
            there = jnp.logical_not(here)
            spot = col & 3

            def put(r, block):
                target[r, p, spot] = block

            @pl.when(here)
            def _():
                for r in range(3):
                    target[r, p, spot] = local[r, p, col]

            @pl.when(jnp.logical_and(there, low))
            def _():
                load_block(p * b + col, 3, put, from_left, in_a, in_b, first)

            @pl.when(jnp.logical_and(there, jnp.logical_not(low)))
            def _():
                slot = (p - n_low) * (8 - b) + col - b
                load_block(slot, 3, put, from_right, in_a, in_b, last)

        for i in range(4):
            move(core * 4 + i, keep)
            move((1 - core) * 4 + i, send)


def temporal_body(arrived, gates, out):
    frames = 8
    tokens = frames * 16

    def spot(dim, shape):
        return lax.broadcasted_iota(jnp.int32, shape, dim) & 15

    mask = spot(0, (tokens, 2 * tokens)) == spot(1, (tokens, 2 * tokens))
    for p in range(8):
        lanes = slice(p * LANES, (p + 1) * LANES)
        q, k, v, g = (arrived[:, 16 * r : 16 * r + 16, lanes] for r in range(4))
        g = (g.astype(F32) * gates[:, :, lanes]).astype(BF16)
        q, k, v, g = (x.reshape(tokens, LANES) for x in (q, k, v, g))
        for r, grad in enumerate(attend(q, k, v, g, mask)):
            out[:, 16 * r : 16 * r + 16, lanes] = grad.astype(BF16).reshape(frames, 16, LANES)


def final_body(scal, keep, got, times, dq, dk, dv):
    core = scal[2]
    for half in range(2):

        @pl.when(core == half)
        def _():
            for r, out in enumerate((dq, dk, dv)):
                for side, part in ((half, keep), (1 - half, got)):
                    for p in range(PAIRS):
                        lo = side * PAIRS * LANES + p * LANES
                        space = part[r, p].astype(F32).reshape(8, 16, LANES)
                        time = times[:, 16 * r : 16 * r + 16, lo : lo + LANES].astype(F32)
                        out[:, lo : lo + LANES] = (space + time).astype(BF16).reshape(128, LANES)


def send(x, by):
    devices = lax.axis_size("lon")
    chips = devices // 2
    moves = [
        (i, ((i // 2 + by[i // 2 % ROW]) % chips) * 2 + i % 2) for i in range(devices) if i // 2 % ROW in by
    ]
    return lax.ppermute(x, "lon", moves)


def scatter_row(cross_b):
    return send(cross_b, {3: -1, 0: 1})


def cross_rows(cross_a, beside):
    return send(cross_a, {3: 1, 0: -1}), send(beside, {2: 2, 1: -2})


def in_row(to_left, to_right):
    return send(to_right, {0: 1, 1: 1, 2: 1}), send(to_left, {1: -1, 2: -1, 3: -1})


def shards(queries, token_keys, values, grad_out, window_shifts, noise_steps, gate_table):
    devices = lax.axis_size("lon")

    def core_swap(x):
        return lax.ppermute(x, "lon", [(i, i ^ 1) for i in range(devices)])

    def over_frames(x):
        return lax.all_to_all(x, "tm", split_axis=0, concat_axis=0, tiled=True)

    frame = lax.axis_index("tm")
    lon = lax.axis_index("lon")
    shift = lax.dynamic_slice_in_dim(window_shifts, frame, 1, 0).reshape(2)
    place = jnp.stack([lon & 1, (lon >> 1) & 3]).astype(jnp.int32)
    scal = jnp.concatenate([shift, place])
    flat = [x.reshape(128, 1024) for x in (queries, token_keys, values, grad_out)]
    half = (4, PAIRS, 4, 32, LANES)

    def sides(count):
        side = (count, SLOTS, 32, LANES)
        return [side, side, (count, HALF, 32, LANES), (count, SLOTS - HALF, 32, LANES)]

    with jax.named_scope("split"):
        stacked, own, other = call(
            split_body, [(8, 64, 1024), half, half], [ANY] * 4, 1 << 20, 3 << 20,
            [pltpu.SemaphoreType.DMA((4, 8))], 60,
        )(*flat)
    arrived = over_frames(stacked)
    got = core_swap(other)
    with jax.named_scope("halo"):
        whole, *out, gates = call(
            halo_body, [(4, PAIRS, 8, 32, LANES)] + sides(4) + [jax.ShapeDtypeStruct((8, 1, 1024), F32)],
            [SMEM] * 2 + [VMEM] * 3, HALO_FLOPS, 3 << 20,
        )(scal, noise_steps, own, got, gate_table)
    to_left, to_right, cross_a, cross_b = out
    beside = scatter_row(cross_b)
    to_left, to_right, beside = lax.optimization_barrier((to_left, to_right, beside))
    from_left, from_right = in_row(to_left, to_right)
    in_a, in_b = cross_rows(cross_a, beside)
    arrived, _ = lax.optimization_barrier((arrived, beside))
    with jax.named_scope("temporal"):
        (out_time,) = call(
            temporal_body, [(8, 48, 1024)], [VMEM, VMEM], TEMPORAL_FLOPS, 4 << 20
        )(arrived, gates)
    times = over_frames(out_time)
    with jax.named_scope("spatial"):
        strips, out_a, out_b = call(
            spatial_body, [(3, PAIRS, 8, 32, LANES)] + sides(3)[2:], [SMEM] + [VMEM] * 5, SPATIAL_FLOPS, 4 << 20,
            [pltpu.VMEM((PAIRS, 4, 8, 32, LANES), BF16)],
        )(scal, whole, from_left, from_right, in_a, in_b)
    beside = scatter_row(out_b)
    out_a, beside = lax.optimization_barrier((out_a, beside))
    in_a, in_b = cross_rows(out_a, beside)
    with jax.named_scope("sides"):
        back_left, back_right = call(sides_body, sides(3)[:2], [SMEM, VMEM], SIDES_FLOPS, 1 << 20)(scal, strips)
    from_left, from_right = in_row(back_left, back_right)
    with jax.named_scope("gather"):
        keep, send = call(
            gather_body, [(3, PAIRS, 4, 32, LANES)] * 2, [SMEM] + [VMEM] * 5, GATHER_FLOPS, 2 << 20
        )(scal, strips, from_left, from_right, in_a, in_b)
    got_back = core_swap(send)
    with jax.named_scope("final"):
        outs = call(final_body, [(128, 1024)] * 3, [SMEM] + [VMEM] * 3, 1 << 20, 3 << 20)(
            scal, keep, got_back, times
        )
    return tuple(x.reshape(1, 4, 32, 1024) for x in outs)


def solution(mesh):
    placed = P("tm", "lon", None, None)
    return jax.shard_map(
        shards,
        mesh=mesh,
        in_specs=(placed, placed, placed, placed, P(), P(), P()),
        out_specs=(placed, placed, placed),
        check_vma=False,
    )
```
